32 devices in a mesh: groups: 2 (over y), gx: 8 (over z, x), gy: 2 (over core).
Axes of the slice: x: 2, y: 2, z: 4, core: 2. Of those that a mesh axis runs over, the one named last changes fastest.
Arguments:
- tokens: bfloat16 [64, 8192], P(('groups', 'gx'), 'gy'), parts along dimension 0, may hold values from -6 to 6
- gate_weight: bfloat16 [3584, 8192], P('gx', 'gy'), may hold values from -0.0625 to 0.0625
- up_weight: bfloat16 [3584, 8192], P('gx', 'gy'), may hold values from -0.0625 to 0.0625
- down_weight: bfloat16 [3584, 8192], P('gx', 'gy'), may hold values from -0.125 to 0.125
Outputs:
- stream: bfloat16 [64, 8192], P(('groups', 'gx'), 'gy'), parts along dimension 0
The draws below stay inside these ranges and needn't reach their ends.
There are 2 independent parts, one for each index of `groups`. The reference program is written for one: setup_inputs(seed, part) draws one part's arguments, and reference() takes and returns one part's arrays. A program takes and returns all parts, laid end to end along the dimension named above; an argument that names none is the same for every part. Nothing has to cross between parts.
All inputs are finite; a program needn't handle non-finite values.
Results may differ from the reference program's by a relative error of at most 0.0075.
Values may be sent and summed in bfloat16 or wider, within the bound.
A program may use at most 64 MiB of HBM per device.

```python
import jax
import jax.numpy as jnp

D = 8192
LAYERS = 2
FF = 3584
ROWS = 32


def with_spikes(array, rng, source, target, shards_of, factor):
    owner, partner = [(jnp.arange(array.shape[position]) // (array.shape[position] // shards_of)).reshape([-1 if axis == position else 1 for axis in range(array.ndim)]) for position in (source, target)]
    chosen = jax.random.permutation(rng, shards_of)[partner]
    strong = (owner == chosen) | (owner == (partner + shards_of // 2) % shards_of)
    return jnp.where(strong, factor * array, array)


def steps_of(rng, shape, cuts, low, high):
    def one(axis_at, parts):
        draws = jax.random.uniform(jax.random.fold_in(jax.random.fold_in(rng, 6), axis_at), (parts,), jnp.float32, low / len(cuts), high / len(cuts))
        return jnp.repeat(jnp.exp(draws), shape[axis_at] // parts).reshape((-1,) + (1,) * (len(shape) - axis_at - 1))

    factor_of = one(*cuts[0])
    for cut in cuts[1:]:
        factor_of = factor_of * one(*cut)
    return factor_of


def scatter_about(key, shape, scale, reach, shards=(), kind=jnp.bfloat16):
    result = jax.random.normal(key, shape, jnp.float32) * scale
    if len(shards) > 0:
        result = steps_of(key, shape, shards, -0.22, 0.18) * result
    return jnp.clip(result, min=-reach, max=reach).astype(kind)


def noise_with(stream_key, extent, deviation, most, pieces, heavy, dtype=jnp.bfloat16):
    entries = deviation * jax.random.normal(stream_key, extent, jnp.float32)
    if pieces:
        entries = entries * steps_of(stream_key, extent, pieces, -0.22, 0.18)
    return jnp.clip(with_spikes(entries, jax.random.fold_in(stream_key, 3), *heavy), -most, most).astype(dtype)


def setup_inputs(seed: int = 0, part: int = 0) -> dict:
    key_list = jax.random.split(jax.random.key(seed), 5)
    part_keys = jax.random.split(jax.random.fold_in(key_list[4], part), 5)
    return {
        "tokens": scatter_about(part_keys[0], (ROWS, D), 1.0, 6.0, ((0, 8), (1, 2))),
        "gate_weight": scatter_about(key_list[1], (FF, D), D ** -0.5, 0.0625, ((0, 8), (1, 2))),
        "up_weight": scatter_about(key_list[2], (FF, D), D ** -0.5, 0.0625, ((0, 8), (1, 2))),
        "down_weight": noise_with(key_list[3], (FF, D), FF ** -0.5, 0.125, ((0, 8), (1, 2)), (0, 1, 8, 2.0)),
    }


def reference(tokens, gate_weight, up_weight, down_weight):
    stream = tokens
    for repeat in range(LAYERS):
        gate_total = jnp.dot(stream, gate_weight.T, preferred_element_type=jnp.float32)
        up_total = jnp.dot(stream, up_weight.T, preferred_element_type=jnp.float32)
        hidden = (jax.nn.silu(gate_total) * up_total).astype(jnp.bfloat16)
        summed = jnp.dot(hidden, down_weight, preferred_element_type=jnp.float32)
        stream = (stream.astype(jnp.float32) + summed).astype(jnp.bfloat16)
    return stream
```

```python
import functools

import jax
import jax.numpy as jnp
from jax import lax
from jax.experimental import pallas as pl
from jax.experimental.pallas import tpu as pltpu
from jax.sharding import PartitionSpec as P

LAYERS = 2
CHUNKS = 4
MESH = pl.DeviceIdType.MESH
F32 = jnp.float32
BF16 = jnp.bfloat16
NT = (((1,), (1,)), ((), ()))


def kernel(n, tokens, wg_hbm, wu_hbm, wd_hbm, out,
           wg, wu, wd, ag, snd, rcv, part, part_in,
           w_sem, tok_sem, ag_send, ag_recv, rs_send, rs_recv, gy_send, gy_recv):
    me = lax.axis_index("gx")
    my_gy = lax.axis_index("gy")
    other = 1 - my_gy
    r, d = tokens.shape
    kc = d // CHUNKS
    rows = n * r

    def cols(c):
        return pl.ds(c * kc, kc)

    loads = []
    for c in range(CHUNKS):
        t = pltpu.make_async_copy(tokens.at[:, cols(c)], ag.at[0, c, me], tok_sem.at[c])
        t.start()
        loads.append(t)
    weights = {}
    for k, (h, v) in enumerate(((wg_hbm, wg), (wu_hbm, wu), (wd_hbm, wd))):
        for c in range(CHUNKS):
            weights[k, c] = pltpu.make_async_copy(h.at[:, cols(c)], v.at[c], w_sem.at[k, c])
    for c in range(CHUNKS):
        weights[0, c].start()
        weights[1, c].start()
    for c in range(CHUNKS):
        weights[2, c].start()

    barrier = pltpu.get_barrier_semaphore()

    def greet(i, carry):
        pl.semaphore_signal(barrier, inc=1, device_id={"gx": lax.rem(me + i, n)}, device_id_type=MESH)
        return carry

    unroll = n <= 8
    lax.fori_loop(1, n, greet, 0, unroll=unroll)
    pl.semaphore_signal(barrier, inc=1, device_id={"gy": other}, device_id_type=MESH)
    for t in loads:
        t.wait()
    pl.semaphore_wait(barrier, n)

    def send_ag(l, c):
        def body(i, carry):
            pltpu.make_async_remote_copy(
                src_ref=ag.at[l, c, me], dst_ref=ag.at[l, c, me],
                send_sem=ag_send.at[l], recv_sem=ag_recv.at[l, c],
                device_id={"gx": lax.rem(me + i, n)}, device_id_type=MESH).start()
            return carry
        lax.fori_loop(1, n, body, 0, unroll=unroll)

    def send_rs(l, c):
        def body(i, carry):
            peer = lax.rem(me + i, n)
            pltpu.make_async_remote_copy(
                src_ref=snd.at[l, c, peer], dst_ref=rcv.at[l, c, me],
                send_sem=rs_send.at[l], recv_sem=rs_recv.at[l, c],
                device_id={"gx": peer}, device_id_type=MESH).start()
            return carry
        lax.fori_loop(1, n, body, 0, unroll=unroll)

    def arrived(buf, sem):
        pltpu.make_async_copy(buf, buf, sem).wait()

    for c in range(CHUNKS):
        send_ag(0, c)

    for l in range(LAYERS):
        gate = up = None
        for c in range(CHUNKS):
            if l == 0:
                weights[0, c].wait()
                weights[1, c].wait()
            arrived(ag.at[l, c, pl.ds(0, n - 1)], ag_recv.at[l, c])
            x = ag[l, c].astype(F32).reshape(rows, kc).astype(BF16)
            g = lax.dot_general(x, wg[c], NT, preferred_element_type=F32)
            u = lax.dot_general(x, wu[c], NT, preferred_element_type=F32)
            gate = g if gate is None else gate + g
            up = u if up is None else up + u
        part[l, 0] = gate
        part[l, 1] = up
        swap = pltpu.make_async_remote_copy(
            src_ref=part.at[l], dst_ref=part_in.at[l],
            send_sem=gy_send.at[l], recv_sem=gy_recv.at[l],
            device_id={"gy": other}, device_id_type=MESH)
        swap.start()
        if l == 0:
            for c in range(CHUNKS):
                weights[2, c].wait()
        swap.wait()
        gate = part[l, 0] + part_in[l, 0]
        up = part[l, 1] + part_in[l, 1]
        hidden = (jax.nn.silu(gate) * up).astype(BF16)
        for c in range(CHUNKS):
            p = jnp.dot(hidden, wd[c], preferred_element_type=F32)
            snd[l, c] = p.reshape(n, r, kc).astype(BF16)
            send_rs(l, c)
            rcv[l, c, me] = snd[l, c, me]
        for c in range(CHUNKS):
            arrived(rcv.at[l, c, pl.ds(0, n - 1)], rs_recv.at[l, c])
            summed = jnp.sum(rcv[l, c].astype(F32), axis=0)
            stream = (ag[l, c, me].astype(F32) + summed).astype(BF16)
            if l + 1 < LAYERS:
                ag[l + 1, c, me] = stream
                send_ag(l + 1, c)
            else:
                out[:, cols(c)] = stream
    for l in range(LAYERS):
        arrived(ag.at[l, :, pl.ds(0, n - 1)], ag_send.at[l])
        arrived(snd.at[l, :, pl.ds(0, n - 1)], rs_send.at[l])


def local(n, tokens, gate_weight, up_weight, down_weight):
    r, d = tokens.shape
    units = gate_weight.shape[0]
    rows = n * r
    kc = d // CHUNKS
    flops = 2 * LAYERS * 3 * rows * units * d
    return pl.pallas_call(
        functools.partial(kernel, n),
        out_shape=jax.ShapeDtypeStruct((r, d), BF16),
        in_specs=[pl.BlockSpec(memory_space=pl.ANY)] * 4,
        out_specs=pl.BlockSpec(memory_space=pltpu.VMEM),
        scratch_shapes=[
            pltpu.VMEM((CHUNKS, units, kc), BF16),
            pltpu.VMEM((CHUNKS, units, kc), BF16),
            pltpu.VMEM((CHUNKS, units, kc), BF16),
            pltpu.VMEM((LAYERS, CHUNKS, n, r, kc), BF16),
            pltpu.VMEM((LAYERS, CHUNKS, n, r, kc), BF16),
            pltpu.VMEM((LAYERS, CHUNKS, n, r, kc), BF16),
            pltpu.VMEM((LAYERS, 2, rows, units), F32),
            pltpu.VMEM((LAYERS, 2, rows, units), F32),
            pltpu.SemaphoreType.DMA((3, CHUNKS)),
            pltpu.SemaphoreType.DMA((CHUNKS,)),
            pltpu.SemaphoreType.DMA((LAYERS,)),
            pltpu.SemaphoreType.DMA((LAYERS, CHUNKS)),
            pltpu.SemaphoreType.DMA((LAYERS,)),
            pltpu.SemaphoreType.DMA((LAYERS, CHUNKS)),
            pltpu.SemaphoreType.DMA((LAYERS,)),
            pltpu.SemaphoreType.DMA((LAYERS,)),
        ],
        compiler_params=pltpu.CompilerParams(
            collective_id=0, has_side_effects=True, vmem_limit_bytes=56 * 1024 * 1024),
        cost_estimate=pl.CostEstimate(
            flops=flops, bytes_accessed=3 * units * d * 2, transcendentals=LAYERS * rows * units),
    )(tokens, gate_weight, up_weight, down_weight)


def solution(mesh):
    n = mesh.shape["gx"]
    return jax.shard_map(
        functools.partial(local, n),
        mesh=mesh,
        in_specs=(P(("groups", "gx"), "gy"), P("gx", "gy"), P("gx", "gy"), P("gx", "gy")),
        out_specs=P(("groups", "gx"), "gy"),
        check_vma=False,
    )
```

```python
import functools

import jax
import jax.numpy as jnp
from jax import lax
from jax.experimental import pallas as pl
from jax.experimental.pallas import tpu as pltpu
from jax.sharding import PartitionSpec as P

LAYERS = 2
CHUNKS = 4
SKEW = 2.5
MESH = pl.DeviceIdType.MESH
F32 = jnp.float32
BF16 = jnp.bfloat16
NT = (((1,), (1,)), ((), ()))


def kernel(n, nx, tokens, wg_hbm, wu_hbm, wd_hbm, out,
           wg, wu, wd, ag, snd, xin, mid, zin, part, part_in,
           w_sem, tok_sem, agz_send, agz_recv, agx_send, agx_recv,
           rsx_send, rsx_recv, rsz_send, rsz_recv, gy_send, gy_recv):
    nz = n // nx
    me = lax.axis_index("gx")
    my_x, my_z = lax.rem(me, nx), lax.div(me, nx)
    other = 1 - lax.axis_index("gy")
    r, d = tokens.shape
    kc = d // CHUNKS
    rows = n * r

    def cols(c):
        return pl.ds(c * kc, kc)

    def at(x, z):
        return {"gx": z * nx + x}

    def z_peers(body):
        def step(i, carry):
            body(lax.rem(my_z + i, nz))
            return carry
        lax.fori_loop(1, nz, step, 0, unroll=nz <= 4)

    def x_peers(body):
        def step(i, carry):
            body(lax.rem(my_x + i, nx))
            return carry
        lax.fori_loop(1, nx, step, 0, unroll=nx <= 4)

    def arrived(buf, sem):
        pltpu.make_async_copy(buf, buf, sem).wait()

    own = [pltpu.make_async_copy(tokens.at[:, cols(c)], ag.at[0, c, my_x, my_z], tok_sem.at[c])
           for c in range(CHUNKS)]
    for t in own:
        t.start()
    weights = {}
    for k, (h, v) in enumerate(((wg_hbm, wg), (wu_hbm, wu), (wd_hbm, wd))):
        for c in range(CHUNKS):
            weights[k, c] = pltpu.make_async_copy(h.at[:, cols(c)], v.at[c], w_sem.at[k, c])
    for c in range(CHUNKS):
        weights[0, c].start()
        weights[1, c].start()
    for c in range(CHUNKS):
        weights[2, c].start()

    barrier = pltpu.get_barrier_semaphore()
    z_peers(lambda z: pl.semaphore_signal(barrier, inc=1, device_id=at(my_x, z), device_id_type=MESH))
    x_peers(lambda x: pl.semaphore_signal(barrier, inc=1, device_id=at(x, my_z), device_id_type=MESH))
    pl.semaphore_signal(barrier, inc=1, device_id={"gy": other}, device_id_type=MESH)
    for t in own:
        t.wait()
    pl.semaphore_wait(barrier, nz + nx - 1)

    def gather_z(l, c):
        z_peers(lambda z: pltpu.make_async_remote_copy(
            src_ref=ag.at[l, c, my_x, my_z], dst_ref=ag.at[l, c, my_x, my_z],
            send_sem=agz_send.at[l], recv_sem=agz_recv.at[l, c],
            device_id=at(my_x, z), device_id_type=MESH).start())

    def gather_x(l, c):
        arrived(ag.at[l, c, 0, pl.ds(0, nz - 1)], agz_recv.at[l, c])
        x_peers(lambda x: pltpu.make_async_remote_copy(
            src_ref=ag.at[l, c, my_x], dst_ref=ag.at[l, c, my_x],
            send_sem=agx_send.at[l], recv_sem=agx_recv.at[l, c],
            device_id=at(x, my_z), device_id_type=MESH).start())

    def gate_up(l, c, acc):
        if l == 0:
            weights[0, c].wait()
            weights[1, c].wait()
        arrived(ag.at[l, c, pl.ds(0, nx - 1)], agx_recv.at[l, c])
        x = ag[l, c].astype(F32).reshape(rows, kc).astype(BF16)
        for k, w in enumerate((wg, wu)):
            v = lax.dot_general(x, w[c], NT, preferred_element_type=F32)
            acc[k] = v if acc[k] is None else acc[k] + v

    def exchange(l, acc):
        part[l, 0] = acc[0]
        part[l, 1] = acc[1]
        swap = pltpu.make_async_remote_copy(
            src_ref=part.at[l], dst_ref=part_in.at[l],
            send_sem=gy_send.at[l], recv_sem=gy_recv.at[l],
            device_id={"gy": other}, device_id_type=MESH)
        swap.start()
        if l == 0:
            for c in range(CHUNKS):
                weights[2, c].wait()
        swap.wait()
        gate = part[l, 0] + part_in[l, 0]
        up = part[l, 1] + part_in[l, 1]
        return (jax.nn.silu(gate) * up).astype(BF16)

    def down(l, c, hidden):
        p = jnp.dot(hidden, wd[c], preferred_element_type=F32)
        snd[l, c] = p.astype(BF16).reshape(nx, nz * r, kc)
        x_peers(lambda x: pltpu.make_async_remote_copy(
            src_ref=snd.at[l, c, x], dst_ref=xin.at[l, c, my_x],
            send_sem=rsx_send.at[l], recv_sem=rsx_recv.at[l, c],
            device_id=at(x, my_z), device_id_type=MESH).start())
        xin[l, c, my_x] = snd[l, c, my_x]

    def scatter_z(l, c):
        arrived(xin.at[l, c, pl.ds(0, nx - 1)], rsx_recv.at[l, c])
        total = jnp.sum(xin[l, c].astype(F32), axis=0)
        mid[l, c] = total.reshape(nz, r, kc).astype(BF16)
        z_peers(lambda z: pltpu.make_async_remote_copy(
            src_ref=mid.at[l, c, z], dst_ref=zin.at[l, c, my_z],
            send_sem=rsz_send.at[l], recv_sem=rsz_recv.at[l, c],
            device_id=at(my_x, z), device_id_type=MESH).start())
        zin[l, c, my_z] = mid[l, c, my_z]

    def update(l, c):
        arrived(zin.at[l, c, pl.ds(0, nz - 1)], rsz_recv.at[l, c])
        summed = jnp.sum(zin[l, c].astype(F32), axis=0)
        stream = (ag[l, c, my_x, my_z].astype(F32) + summed).astype(BF16)
        if l + 1 < LAYERS:
            ag[l + 1, c, my_x, my_z] = stream
            gather_z(l + 1, c)
        else:
            out[:, cols(c)] = stream

    for c in range(CHUNKS):
        gather_z(0, c)
    for l in range(LAYERS + 1):
        stages = []
        if l > 0:
            stages += [lambda c: scatter_z(l - 1, c), lambda c: update(l - 1, c)]
            for c in range(CHUNKS):
                down(l - 1, c, hidden)
        if l < LAYERS:
            acc = [None, None]
            stages += [lambda c: gather_x(l, c), lambda c: gate_up(l, c, acc)]
        order = sorted((k * SKEW + c, -k, k, c) for k in range(len(stages)) for c in range(CHUNKS))
        for _, _, k, c in order:
            stages[k](c)
        if l < LAYERS:
            hidden = exchange(l, acc)
    for l in range(LAYERS):
        arrived(ag.at[l, :, 0, pl.ds(0, nz - 1)], agz_send.at[l])
        arrived(ag.at[l, :, pl.ds(0, nx - 1)], agx_send.at[l])
        arrived(snd.at[l, :, pl.ds(0, nx - 1)], rsx_send.at[l])
        arrived(mid.at[l, :, pl.ds(0, nz - 1)], rsz_send.at[l])


def columns_of(n):
    nx = 2
    while nx ** 3 < n:
        nx *= 2
    return nx


def local(n, tokens, gate_weight, up_weight, down_weight):
    r, d = tokens.shape
    units = gate_weight.shape[0]
    rows = n * r
    nx = columns_of(n)
    nz = n // nx
    kc = d // CHUNKS
    flops = 2 * LAYERS * 3 * rows * units * d
    return pl.pallas_call(
        functools.partial(kernel, n, nx),
        out_shape=jax.ShapeDtypeStruct((r, d), BF16),
        in_specs=[pl.BlockSpec(memory_space=pl.ANY)] * 4,
        out_specs=pl.BlockSpec(memory_space=pltpu.VMEM),
        scratch_shapes=[
            pltpu.VMEM((CHUNKS, units, kc), BF16),
            pltpu.VMEM((CHUNKS, units, kc), BF16),
            pltpu.VMEM((CHUNKS, units, kc), BF16),
            pltpu.VMEM((LAYERS, CHUNKS, nx, nz, r, kc), BF16),
            pltpu.VMEM((LAYERS, CHUNKS, nx, nz * r, kc), BF16),
            pltpu.VMEM((LAYERS, CHUNKS, nx, nz * r, kc), BF16),
            pltpu.VMEM((LAYERS, CHUNKS, nz, r, kc), BF16),
            pltpu.VMEM((LAYERS, CHUNKS, nz, r, kc), BF16),
            pltpu.VMEM((LAYERS, 2, rows, units), F32),
            pltpu.VMEM((LAYERS, 2, rows, units), F32),
            pltpu.SemaphoreType.DMA((3, CHUNKS)),
            pltpu.SemaphoreType.DMA((CHUNKS,)),
            pltpu.SemaphoreType.DMA((LAYERS,)),
            pltpu.SemaphoreType.DMA((LAYERS, CHUNKS)),
            pltpu.SemaphoreType.DMA((LAYERS,)),
            pltpu.SemaphoreType.DMA((LAYERS, CHUNKS)),
            pltpu.SemaphoreType.DMA((LAYERS,)),
            pltpu.SemaphoreType.DMA((LAYERS, CHUNKS)),
            pltpu.SemaphoreType.DMA((LAYERS,)),
            pltpu.SemaphoreType.DMA((LAYERS, CHUNKS)),
            pltpu.SemaphoreType.DMA((LAYERS,)),
            pltpu.SemaphoreType.DMA((LAYERS,)),
        ],
        compiler_params=pltpu.CompilerParams(
            collective_id=0, has_side_effects=True, vmem_limit_bytes=56 * 1024 * 1024),
        cost_estimate=pl.CostEstimate(
            flops=flops, bytes_accessed=3 * units * d * 2, transcendentals=LAYERS * rows * units),
    )(tokens, gate_weight, up_weight, down_weight)


def solution(mesh):
    n = mesh.shape["gx"]
    return jax.shard_map(
        functools.partial(local, n),
        mesh=mesh,
        in_specs=(P(("groups", "gx"), "gy"), P("gx", "gy"), P("gx", "gy"), P("gx", "gy")),
        out_specs=P(("groups", "gx"), "gy"),
        check_vma=False,
    )
```

```python
import functools

import jax
import jax.numpy as jnp
from jax import lax
from jax.experimental import pallas as pl
from jax.experimental.pallas import tpu as pltpu
from jax.sharding import PartitionSpec as P

LAYERS = 2
CHUNKS = 4
MESH = pl.DeviceIdType.MESH
F32 = jnp.float32
BF16 = jnp.bfloat16
NT = (((1,), (1,)), ((), ()))


def kernel(n, tokens, wg_hbm, wu_hbm, wd_hbm, out,
           wg, wu, wd, ag, snd, rcv, part, part_in,
           w_sem, tok_sem, ag_send, ag_recv, rs_send, rs_recv, gy_send, gy_recv):
    me = lax.axis_index("gx")
    my_gy = lax.axis_index("gy")
    other = 1 - my_gy
    r, d = tokens.shape
    kc = d // CHUNKS
    rows = n * r

    def cols(c):
        return pl.ds(c * kc, kc)

    loads = []
    for c in range(CHUNKS):
        t = pltpu.make_async_copy(tokens.at[:, cols(c)], ag.at[0, c, me], tok_sem.at[c])
        t.start()
        loads.append(t)
    weights = {}
    for k, (h, v) in enumerate(((wg_hbm, wg), (wu_hbm, wu), (wd_hbm, wd))):
        for c in range(CHUNKS):
            weights[k, c] = pltpu.make_async_copy(h.at[:, cols(c)], v.at[c], w_sem.at[k, c])
    for c in range(CHUNKS):
        weights[0, c].start()
        weights[1, c].start()
    for c in range(CHUNKS):
        weights[2, c].start()

    barrier = pltpu.get_barrier_semaphore()

    def greet(i, carry):
        pl.semaphore_signal(barrier, inc=1, device_id={"gx": lax.rem(me + i, n)}, device_id_type=MESH)
        return carry

    unroll = n <= 8
    lax.fori_loop(1, n, greet, 0, unroll=unroll)
    pl.semaphore_signal(barrier, inc=1, device_id={"gy": other}, device_id_type=MESH)
    for t in loads:
        t.wait()
    pl.semaphore_wait(barrier, n)

    def flipped(k):
        peer, bit = me, 1
        while bit <= k:
            if k & bit:
                peer = peer + bit - 2 * bit * lax.rem(lax.div(me, bit), 2)
            bit *= 2
        return peer

    def peers(body):
        if n <= 8:
            for k in range(n - 1, 0, -1):
                body(flipped(k))
        else:
            def step(i, carry):
                body(lax.rem(me + i, n))
                return carry
            lax.fori_loop(1, n, step, 0)

    def send_ag(l, c):
        def body(peer):
            pltpu.make_async_remote_copy(
                src_ref=ag.at[l, c, me], dst_ref=ag.at[l, c, me],
                send_sem=ag_send.at[l], recv_sem=ag_recv.at[l, c],
                device_id={"gx": peer}, device_id_type=MESH).start()
        peers(body)

    def send_rs(l, c):
        def body(peer):
            pltpu.make_async_remote_copy(
                src_ref=snd.at[l, c, peer], dst_ref=rcv.at[l, c, me],
                send_sem=rs_send.at[l], recv_sem=rs_recv.at[l, c],
                device_id={"gx": peer}, device_id_type=MESH).start()
        peers(body)

    def arrived(buf, sem):
        pltpu.make_async_copy(buf, buf, sem).wait()

    for c in range(CHUNKS):
        send_ag(0, c)

    for l in range(LAYERS):
        gate = up = None
        for c in range(CHUNKS):
            if l == 0:
                weights[0, c].wait()
                weights[1, c].wait()
            arrived(ag.at[l, c, pl.ds(0, n - 1)], ag_recv.at[l, c])
            x = ag[l, c].astype(F32).reshape(rows, kc).astype(BF16)
            g = lax.dot_general(x, wg[c], NT, preferred_element_type=F32)
            u = lax.dot_general(x, wu[c], NT, preferred_element_type=F32)
            gate = g if gate is None else gate + g
            up = u if up is None else up + u
        part[l, 0] = gate
        part[l, 1] = up
        swap = pltpu.make_async_remote_copy(
            src_ref=part.at[l], dst_ref=part_in.at[l],
            send_sem=gy_send.at[l], recv_sem=gy_recv.at[l],
            device_id={"gy": other}, device_id_type=MESH)
        swap.start()
        if l == 0:
            for c in range(CHUNKS):
                weights[2, c].wait()
        swap.wait()
        gate = part[l, 0] + part_in[l, 0]
        up = part[l, 1] + part_in[l, 1]
        hidden = (jax.nn.silu(gate) * up).astype(BF16)
        for c in range(CHUNKS):
            p = jnp.dot(hidden, wd[c], preferred_element_type=F32)
            snd[l, c] = p.reshape(n, r, kc).astype(BF16)
            send_rs(l, c)
            rcv[l, c, me] = snd[l, c, me]
        for c in range(CHUNKS):
            arrived(rcv.at[l, c, pl.ds(0, n - 1)], rs_recv.at[l, c])
            summed = jnp.sum(rcv[l, c].astype(F32), axis=0)
            stream = (ag[l, c, me].astype(F32) + summed).astype(BF16)
            if l + 1 < LAYERS:
                ag[l + 1, c, me] = stream
                send_ag(l + 1, c)
            else:
                out[:, cols(c)] = stream
    for l in range(LAYERS):
        arrived(ag.at[l, :, pl.ds(0, n - 1)], ag_send.at[l])
        arrived(snd.at[l, :, pl.ds(0, n - 1)], rs_send.at[l])


def local(n, tokens, gate_weight, up_weight, down_weight):
    r, d = tokens.shape
    units = gate_weight.shape[0]
    rows = n * r
    kc = d // CHUNKS
    flops = 2 * LAYERS * 3 * rows * units * d
    return pl.pallas_call(
        functools.partial(kernel, n),
        out_shape=jax.ShapeDtypeStruct((r, d), BF16),
        in_specs=[pl.BlockSpec(memory_space=pl.ANY)] * 4,
        out_specs=pl.BlockSpec(memory_space=pltpu.VMEM),
        scratch_shapes=[
            pltpu.VMEM((CHUNKS, units, kc), BF16),
            pltpu.VMEM((CHUNKS, units, kc), BF16),
            pltpu.VMEM((CHUNKS, units, kc), BF16),
            pltpu.VMEM((LAYERS, CHUNKS, n, r, kc), BF16),
            pltpu.VMEM((LAYERS, CHUNKS, n, r, kc), BF16),
            pltpu.VMEM((LAYERS, CHUNKS, n, r, kc), BF16),
            pltpu.VMEM((LAYERS, 2, rows, units), F32),
            pltpu.VMEM((LAYERS, 2, rows, units), F32),
            pltpu.SemaphoreType.DMA((3, CHUNKS)),
            pltpu.SemaphoreType.DMA((CHUNKS,)),
            pltpu.SemaphoreType.DMA((LAYERS,)),
            pltpu.SemaphoreType.DMA((LAYERS, CHUNKS)),
            pltpu.SemaphoreType.DMA((LAYERS,)),
            pltpu.SemaphoreType.DMA((LAYERS, CHUNKS)),
            pltpu.SemaphoreType.DMA((LAYERS,)),
            pltpu.SemaphoreType.DMA((LAYERS,)),
        ],
        compiler_params=pltpu.CompilerParams(
            collective_id=0, has_side_effects=True, vmem_limit_bytes=56 * 1024 * 1024),
        cost_estimate=pl.CostEstimate(
            flops=flops, bytes_accessed=3 * units * d * 2, transcendentals=LAYERS * rows * units),
    )(tokens, gate_weight, up_weight, down_weight)


def solution(mesh):
    n = mesh.shape["gx"]
    return jax.shard_map(
        functools.partial(local, n),
        mesh=mesh,
        in_specs=(P(("groups", "gx"), "gy"), P("gx", "gy"), P("gx", "gy"), P("gx", "gy")),
        out_specs=P(("groups", "gx"), "gy"),
        check_vma=False,
    )
```

```python
import functools

import jax
import jax.numpy as jnp
from jax import lax
from jax.experimental import pallas as pl
from jax.experimental.pallas import tpu as pltpu
from jax.sharding import PartitionSpec as P

LAYERS = 2
CHUNKS = 4
MESH = pl.DeviceIdType.MESH
F32 = jnp.float32
BF16 = jnp.bfloat16
NT = (((1,), (1,)), ((), ()))


def kernel(n, tokens, wg_hbm, wu_hbm, wd_hbm, out,
           wg, wu, wd, ag, snd, rcv, part, part_in,
           w_sem, tok_sem, ag_send, ag_recv, rs_send, rs_recv, gy_send, gy_recv):
    me = lax.axis_index("gx")
    my_gy = lax.axis_index("gy")
    other = 1 - my_gy
    r, d = tokens.shape
    kc = d // CHUNKS
    rows = n * r

    def cols(c):
        return pl.ds(c * kc, kc)

    def flipped(k):
        peer, bit = me, 1
        while bit <= k:
            if k & bit:
                peer = peer + bit - 2 * bit * lax.rem(lax.div(me, bit), 2)
            bit *= 2
        return peer

    def peers(body):
        if n <= 8:
            for k in range(n - 1, 0, -1):
                body(flipped(k))
        else:
            def step(i, carry):
                body(lax.rem(me + i, n))
                return carry
            lax.fori_loop(1, n, step, 0)

    barrier = pltpu.get_barrier_semaphore()
    peers(lambda peer: pl.semaphore_signal(
        barrier, inc=1, device_id={"gx": peer}, device_id_type=MESH))
    pl.semaphore_signal(barrier, inc=1, device_id={"gy": other}, device_id_type=MESH)
    loads = []
    for c in range(CHUNKS):
        t = pltpu.make_async_copy(tokens.at[:, cols(c)], ag.at[0, c, me], tok_sem.at[c])
        t.start()
        loads.append(t)
    weights = {}
    for k, (h, v) in enumerate(((wg_hbm, wg), (wu_hbm, wu), (wd_hbm, wd))):
        for c in range(CHUNKS):
            weights[k, c] = pltpu.make_async_copy(h.at[:, cols(c)], v.at[c], w_sem.at[k, c])
    for c in range(CHUNKS):
        weights[0, c].start()
        weights[1, c].start()
    for c in range(CHUNKS):
        weights[2, c].start()

    for t in loads:
        t.wait()
    pl.semaphore_wait(barrier, n)

    def send_ag(l, c):
        def body(peer):
            pltpu.make_async_remote_copy(
                src_ref=ag.at[l, c, me], dst_ref=ag.at[l, c, me],
                send_sem=ag_send.at[l], recv_sem=ag_recv.at[l, c],
                device_id={"gx": peer}, device_id_type=MESH).start()
        peers(body)

    def send_rs(l, c):
        def body(peer):
            pltpu.make_async_remote_copy(
                src_ref=snd.at[l, c, peer], dst_ref=rcv.at[l, c, me],
                send_sem=rs_send.at[l], recv_sem=rs_recv.at[l, c],
                device_id={"gx": peer}, device_id_type=MESH).start()
        peers(body)

    def arrived(buf, sem):
        pltpu.make_async_copy(buf, buf, sem).wait()

    for c in range(CHUNKS):
        send_ag(0, c)

    for l in range(LAYERS):
        gate = up = None
        for c in range(CHUNKS):
            if l == 0:
                weights[0, c].wait()
                weights[1, c].wait()
            arrived(ag.at[l, c, pl.ds(0, n - 1)], ag_recv.at[l, c])
            x = ag[l, c].astype(F32).reshape(rows, kc).astype(BF16)
            g = lax.dot_general(x, wg[c], NT, preferred_element_type=F32)
            u = lax.dot_general(x, wu[c], NT, preferred_element_type=F32)
            gate = g if gate is None else gate + g
            up = u if up is None else up + u
        part[l, 0] = gate
        part[l, 1] = up
        swap = pltpu.make_async_remote_copy(
            src_ref=part.at[l], dst_ref=part_in.at[l],
            send_sem=gy_send.at[l], recv_sem=gy_recv.at[l],
            device_id={"gy": other}, device_id_type=MESH)
        swap.start()
        if l == 0:
            for c in range(CHUNKS):
                weights[2, c].wait()
        swap.wait()
        gate = part[l, 0] + part_in[l, 0]
        up = part[l, 1] + part_in[l, 1]
        hidden = (jax.nn.silu(gate) * up).astype(BF16)
        for c in range(CHUNKS):
            p = jnp.dot(hidden, wd[c], preferred_element_type=F32)
            snd[l, c] = p.reshape(n, r, kc).astype(BF16)
            send_rs(l, c)
            rcv[l, c, me] = snd[l, c, me]
        for c in range(CHUNKS):
            arrived(rcv.at[l, c, pl.ds(0, n - 1)], rs_recv.at[l, c])
            summed = jnp.sum(rcv[l, c].astype(F32), axis=0)
            stream = (ag[l, c, me].astype(F32) + summed).astype(BF16)
            if l + 1 < LAYERS:
                ag[l + 1, c, me] = stream
                send_ag(l + 1, c)
            else:
                out[:, cols(c)] = stream
    for l in range(LAYERS):
        arrived(ag.at[l, :, pl.ds(0, n - 1)], ag_send.at[l])
        arrived(snd.at[l, :, pl.ds(0, n - 1)], rs_send.at[l])


def local(n, tokens, gate_weight, up_weight, down_weight):
    r, d = tokens.shape
    units = gate_weight.shape[0]
    rows = n * r
    kc = d // CHUNKS
    flops = 2 * LAYERS * 3 * rows * units * d
    return pl.pallas_call(
        functools.partial(kernel, n),
        out_shape=jax.ShapeDtypeStruct((r, d), BF16),
        in_specs=[pl.BlockSpec(memory_space=pl.ANY)] * 4,
        out_specs=pl.BlockSpec(memory_space=pltpu.VMEM),
        scratch_shapes=[
            pltpu.VMEM((CHUNKS, units, kc), BF16),
            pltpu.VMEM((CHUNKS, units, kc), BF16),
            pltpu.VMEM((CHUNKS, units, kc), BF16),
            pltpu.VMEM((LAYERS, CHUNKS, n, r, kc), BF16),
            pltpu.VMEM((LAYERS, CHUNKS, n, r, kc), BF16),
            pltpu.VMEM((LAYERS, CHUNKS, n, r, kc), BF16),
            pltpu.VMEM((LAYERS, 2, rows, units), F32),
            pltpu.VMEM((LAYERS, 2, rows, units), F32),
            pltpu.SemaphoreType.DMA((3, CHUNKS)),
            pltpu.SemaphoreType.DMA((CHUNKS,)),
            pltpu.SemaphoreType.DMA((LAYERS,)),
            pltpu.SemaphoreType.DMA((LAYERS, CHUNKS)),
            pltpu.SemaphoreType.DMA((LAYERS,)),
            pltpu.SemaphoreType.DMA((LAYERS, CHUNKS)),
            pltpu.SemaphoreType.DMA((LAYERS,)),
            pltpu.SemaphoreType.DMA((LAYERS,)),
        ],
        compiler_params=pltpu.CompilerParams(
            collective_id=0, has_side_effects=True, vmem_limit_bytes=56 * 1024 * 1024),
        cost_estimate=pl.CostEstimate(
            flops=flops, bytes_accessed=3 * units * d * 2, transcendentals=LAYERS * rows * units),
    )(tokens, gate_weight, up_weight, down_weight)


def solution(mesh):
    n = mesh.shape["gx"]
    return jax.shard_map(
        functools.partial(local, n),
        mesh=mesh,
        in_specs=(P(("groups", "gx"), "gy"), P("gx", "gy"), P("gx", "gy"), P("gx", "gy")),
        out_specs=P(("groups", "gx"), "gy"),
        check_vma=False,
    )
```
